32 devices in a mesh: dp: 8 (over z, y), owner: 4 (over x, core).
Axes of the slice: x: 2, y: 2, z: 4, core: 2. Of those that a mesh axis runs over, the one named last changes fastest.
Arguments:
- tokens: bfloat16 [1024, 4096], P('dp'), may hold values from -6 to 6
- act_basis: bfloat16 [2, 4096, 4096], P(None, 'dp', 'owner'), may hold values from -0.09375 to 0.09375
- grad_basis: bfloat16 [2, 8192, 8192], P(None, 'owner', 'dp'), may hold values from -0.0625 to 0.0625
- grads: bfloat16 [2, 1024, 8192], P(None, 'dp', 'owner'), may hold values from -6 to 6
- expert_ids: int32 [1024, 2], P('dp'), may hold values from 0 to 7, all different within a row; in each aligned block of 128 rows (0 to 127, 128 to 255, ...) at most 64 rows name the same one
Outputs:
- corrected: float32 [2, 8192, 4096], P(None, 'dp', 'owner')
The draws below stay inside these ranges and needn't reach their ends.
Inputs may be any that keep to these rules, and one draw needn't show every extreme that they name: `expert_ids`: among the 128 rows of one device no expert is named by more than 64 rows, a bound that some block reaches; the two experts of a row differ.
All inputs are finite; a program needn't handle non-finite values.
Results may differ from the reference program's by a relative error of at most 0.0013.
Values may be sent and summed in bfloat16 or wider, within the bound.
A program may use at most 128 MiB of HBM per device.

```python
import math
import jax
import jax.numpy as jnp
import numpy as np

D = 4096
EXPERTS = 8
TOPK = 2
FF_WIN = 8192
EXP_WIN = 2
TOK_DEV = 128
CAP = 64
ROWS = 512
TOKENS = 1024
N_DP = 8


def block_scale(stream_key, extent, shards, smallest, largest):
    loudness, own = 1.0, jax.random.fold_in(stream_key, 6)
    for axis_at, shards_of in shards:
        steps = jnp.exp(jax.random.uniform(jax.random.fold_in(own, axis_at), (shards_of,), jnp.float32, smallest / len(shards), largest / len(shards)))
        loudness = loudness * jnp.repeat(steps, extent[axis_at] // shards_of).reshape([-1 if axis == axis_at else 1 for axis in range(len(extent))])
    return loudness


def deal_out(own_key, own, number, rows, number_of, top, most, skew):
    order = jax.random.permutation(own_key, number_of)
    packed, common = load_shares(number_of, rows * top, most, skew, True), load_shares(number_of, rows * top, most, skew, False)
    places = jnp.arange(number_of)

    def named(tallies, offset_by):
        used = int((tallies > 0).sum())
        fixed = max(1, used // 4)
        passed = fixed + (places - fixed + offset_by * (used - fixed)) % max(1, number_of - fixed)
        return jnp.zeros((number_of,), jnp.int32).at[order[jnp.where(places < fixed, places, passed)]].set(jnp.asarray(tallies, jnp.int32))

    tallies = jnp.where(number % 4 == 0, named(packed, number // 4), named(common, number - number // 4 - 1))
    mixed = jax.random.permutation(jax.random.fold_in(own, 3), number_of)
    source_of, taker = mixed[0:number_of // 2 * 2:2], mixed[1:number_of // 2 * 2:2]
    margin = jnp.minimum(tallies[source_of] - 1, most - tallies[taker]) // 2
    margin = jnp.where((source_of == order[0]) | (taker == order[0]) | (tallies[taker] == 0), 0, jnp.maximum(margin, 0))
    passed = jax.random.randint(jax.random.fold_in(own, 4), (number_of // 2,), 0, 1 << 20) % (margin + 1)
    tallies = tallies.at[source_of].add(-passed).at[taker].add(passed)
    labels = jnp.searchsorted(jnp.cumsum(tallies), jnp.arange(rows * top), side="right").astype(jnp.int32)
    table = labels.reshape(top, rows).T
    table = table[jax.random.permutation(jax.random.fold_in(own, 1), rows)]
    offset_by = jax.random.randint(jax.random.fold_in(own, 2), (rows, 1), 0, top)
    return jnp.take_along_axis(table, (jnp.arange(top)[None, :] + offset_by) % top, axis=1)


def load_shares(count, total, reach, lean, full):
    portions = [(1 << 20) // math.isqrt(grade ** lean) + 1 for grade in range(1, count + 1)]
    largest = reach if full else min(reach, max(-(-total // count), total * portions[0] // sum(portions)))
    least = 1 if total - largest >= count - 1 else 0
    given, spare = [largest] + [least] * (count - 1), total - largest - least * (count - 1)
    while spare > 0:
        candidates = [i for i in range(1, count) if given[i] < largest] or [i for i in range(1, count) if given[i] < reach]
        whole, left = sum([portions[i] for i in candidates]), spare
        for i in candidates:
            extra = min(reach - given[i], max(1, left * portions[i] // whole), spare)
            given[i] = given[i] + extra
            spare = spare - extra
    return np.array(given)


def centred(stream_key, shape, scale, limit, split=(), kind=jnp.bfloat16):
    entries = scale * jax.random.normal(stream_key, shape, jnp.float32)
    if split:
        entries = entries * block_scale(stream_key, shape, split, -0.22, 0.18)
    return jnp.clip(entries, -limit, limit).astype(kind)


def setup_inputs(seed: int = 0) -> dict:
    keys = jax.random.split(jax.random.key(seed), 6)
    tokens = centred(keys[0], (TOKENS, D), 1.0, 6.0, ((0, 8),))
    act_basis = centred(keys[1], (EXP_WIN, D, D), D ** -0.5, 0.09375, ((1, 8), (2, 4)))
    grad_basis = centred(keys[2], (EXP_WIN, FF_WIN, FF_WIN), FF_WIN ** -0.5, 0.0625, ((1, 4), (2, 8)))
    grads = centred(keys[3], (EXP_WIN, TOKENS, FF_WIN), 1.0, 6.0, ((1, 8), (2, 4)))
    expert_ids_keys = jax.random.split(jax.random.fold_in(keys[4], 1), TOKENS // TOK_DEV)
    expert_ids_turns = jax.random.permutation(jax.random.fold_in(keys[4], 3), TOKENS // TOK_DEV)
    expert_ids = jax.vmap(lambda own, number: deal_out(jax.random.fold_in(keys[4], 2), own, number, TOK_DEV, EXPERTS, TOPK, CAP, 2))(expert_ids_keys, expert_ids_turns).reshape((TOKENS, TOPK))
    return dict(tokens=tokens, act_basis=act_basis, grad_basis=grad_basis, grads=grads, expert_ids=expert_ids)


def reference(tokens, act_basis, grad_basis, grads, expert_ids):
    token_groups = tokens.reshape(N_DP, TOK_DEV, D).astype(jnp.float32)
    id_groups = expert_ids.reshape(N_DP, TOK_DEV, TOPK)
    slot_order = jnp.arange(CAP, dtype=jnp.int32)
    results = []
    for expert in range(EXP_WIN):
        routed = jnp.any(id_groups == expert, axis=2)
        slot_index = jnp.cumsum(routed.astype(jnp.int32), axis=1) - 1
        chooser = jnp.logical_and(routed[:, None, :], slot_index[:, None, :] == slot_order[None, :, None]).astype(jnp.float32)
        picked_act = jnp.einsum('gct,gtd->gcd', chooser, token_groups).reshape(ROWS, D).astype(jnp.bfloat16)
        grad_groups = grads[expert].reshape(N_DP, TOK_DEV, FF_WIN).astype(jnp.float32)
        picked_grad = jnp.einsum('gct,gtf->gcf', chooser, grad_groups).reshape(ROWS, FF_WIN).astype(jnp.bfloat16)
        act_proj = jnp.dot(picked_act, act_basis[expert], preferred_element_type=jnp.float32).astype(jnp.bfloat16)
        grad_proj = jnp.dot(picked_grad, grad_basis[expert], preferred_element_type=jnp.float32)
        act_sq = jnp.square(act_proj.astype(jnp.float32)).astype(jnp.bfloat16)
        grad_sq = jnp.square(grad_proj).astype(jnp.bfloat16)
        results.append(jnp.dot(grad_sq.T, act_sq, preferred_element_type=jnp.float32) / TOKENS)
    return jnp.stack(results)
```

```python
import jax
import jax.numpy as jnp
from jax import lax
from jax.sharding import PartitionSpec as P


def compact(expert_ids, tokens, grads, capacity):
    slot_order = jnp.arange(capacity, dtype=jnp.int32)[:, None]
    choosers = []
    for expert in range(grads.shape[0]):
        routed = jnp.any(expert_ids == expert, axis=1)
        slot_index = jnp.cumsum(routed.astype(jnp.int32)) - 1
        chosen = jnp.logical_and(routed[None, :], slot_index[None, :] == slot_order)
        choosers.append(chosen.astype(jnp.bfloat16))
    chooser = jnp.stack(choosers)
    picked_act = jnp.einsum(
        "ect,td->ecd", chooser, tokens, preferred_element_type=jnp.float32
    ).astype(jnp.bfloat16)
    picked_grad = jnp.einsum(
        "ect,etf->ecf", chooser, grads, preferred_element_type=jnp.float32
    ).astype(jnp.bfloat16)
    return (picked_act, picked_grad)


def per_device(tokens, act_basis, grad_basis, grads, expert_ids):
    tok_rows = tokens.shape[0]
    capacity = tok_rows // 2
    token_total = tok_rows * lax.axis_size("dp")
    picked_act, picked_grad = compact(expert_ids, tokens, grads, capacity)
    grad_rows = lax.all_gather(picked_grad, "dp", axis=1, tiled=True)
    act_rows = lax.all_to_all(picked_act, "dp", split_axis=2, concat_axis=1, tiled=True)
    act_part = jnp.einsum("ern,ena->era", act_rows, act_basis, preferred_element_type=jnp.float32)
    act_own = lax.psum_scatter(act_part, "dp", scatter_dimension=1, tiled=True).astype(jnp.bfloat16)
    act_all = lax.all_gather(act_own, "dp", axis=1, tiled=True)
    act_sq = jnp.square(act_all.astype(jnp.float32)).astype(jnp.bfloat16)
    grad_part = jnp.einsum("erf,efk->erk", grad_rows, grad_basis, preferred_element_type=jnp.float32)
    grad_own = lax.psum_scatter(grad_part, "owner", scatter_dimension=1, tiled=True)
    grad_sq = lax.all_gather(jnp.square(grad_own).astype(jnp.bfloat16), "owner", axis=1, tiled=True)
    return (
        jnp.einsum("erk,era->eka", grad_sq, act_sq, preferred_element_type=jnp.float32)
        / token_total
    )


def solution(mesh):
    placed = (
        P("dp", None),
        P(None, "dp", "owner"),
        P(None, "owner", "dp"),
        P(None, "dp", "owner"),
        P("dp", None),
    )
    return jax.shard_map(
        per_device, mesh=mesh, in_specs=placed, out_specs=P(None, "dp", "owner"), check_vma=False
    )
```

```python
import functools

import jax
import jax.numpy as jnp
from jax import lax
from jax.experimental import pallas as pl
from jax.experimental.pallas import tpu as pltpu
from jax.sharding import PartitionSpec as P

MESH = pl.DeviceIdType.MESH
RIGHT, LEFT = 0, 1


def compact(expert_ids, tokens, grads, capacity):
    slot_order = jnp.arange(capacity, dtype=jnp.int32)[:, None]
    choosers = []
    for expert in range(grads.shape[0]):
        routed = jnp.any(expert_ids == expert, axis=1)
        slot_index = jnp.cumsum(routed.astype(jnp.int32)) - 1
        chosen = jnp.logical_and(routed[None, :], slot_index[None, :] == slot_order)
        choosers.append(chosen.astype(jnp.bfloat16))
    chooser = jnp.stack(choosers)
    picked_act = jnp.einsum(
        "ect,td->ecd", chooser, tokens, preferred_element_type=jnp.float32
    ).astype(jnp.bfloat16)
    picked_grad = jnp.einsum(
        "ect,etf->ecf", chooser, grads, preferred_element_type=jnp.float32
    ).astype(jnp.bfloat16)
    return (picked_act, picked_grad)


def ring_place(index, size):
    return jnp.where(lax.rem(index, 2) == 0, index // 2, size - 1 - index // 2)


def ring_index(place, size):
    place = lax.rem(place + 2 * size, size)
    return jnp.where(place < size // 2, 2 * place, 2 * (size - 1 - place) + 1)


def exchange_kernel(
    n, m, share, picked_act, picked_grad, act_basis, grad_basis, act_sq, grad_sq,
    act_w, grad_w, rows_in, part, sums, grad_all, grad_part, grad_in,
    load_sem, tok_send, tok_recv, share_send, share_recv, sum_send, sum_recv,
    grad_send, grad_recv, act_send, act_recv, part_send, part_recv, sq_send, sq_recv,
):
    half = n // 2
    experts, cap, _ = picked_grad.shape
    feats = act_basis.shape[1]
    columns = grad_basis.shape[2]
    act_columns = act_basis.shape[2]
    me = lax.axis_index("dp")
    mine = lax.axis_index("owner")
    place = ring_place(me, n)
    towards = (ring_index(place + 1, n), ring_index(place - 1, n))

    def rows(index):
        return pl.ds(pl.multiple_of(index * cap, cap), cap)

    def remote(src, dst, send, recv, **device):
        return pltpu.make_async_remote_copy(
            src_ref=src, dst_ref=dst, send_sem=send, recv_sem=recv,
            device_id=device, device_id_type=MESH,
        )

    load_act = pltpu.make_async_copy(act_basis, act_w, load_sem.at[0])
    load_grad = pltpu.make_async_copy(grad_basis, grad_w, load_sem.at[1])
    load_grad.start()
    load_act.start()

    barrier = pltpu.get_barrier_semaphore()

    @pl.loop(1, n)
    def _(k):
        pl.semaphore_signal(barrier, inc=1, device_id={"dp": lax.rem(me + k, n)}, device_id_type=MESH)

    @pl.loop(1, m)
    def _(k):
        pl.semaphore_signal(barrier, inc=1, device_id={"owner": lax.rem(mine + k, m)}, device_id_type=MESH)

    pl.semaphore_wait(barrier, n + m - 2)

    share_rows = experts * cap // share
    my_share = lax.rem(mine, share)
    share_base = mine - my_share
    my_rows = pl.ds(pl.multiple_of(my_share * share_rows, share_rows), share_rows)

    def features(index):
        return pl.ds(pl.multiple_of(index * feats, feats), feats)

    def token_copy(k):
        to = lax.rem(me + k, n)
        return remote(
            picked_act.at[my_rows, features(to)], rows_in.at[me, my_rows, :],
            tok_send.at[k], tok_recv.at[k], dp=to,
        )

    @pl.loop(1, n)
    def _(k):
        token_copy(k).start()

    own_rows = pltpu.make_async_copy(
        picked_act.at[my_rows, features(me)], rows_in.at[me, my_rows, :], load_sem.at[2]
    )
    own_rows.start()

    def gather_has(way, step, e):
        return step < half - 1 or (step == half - 1 and e % 2 == way)

    def gather_copy(buf, own, send, recv, way, step, e):
        chunk = rows(ring_index(place - step if way == RIGHT else place + step, n))
        src = own.at[e] if own is not None and step == 0 else buf.at[e, chunk, :]
        return remote(
            src, buf.at[e, chunk, :], send.at[way, step, e], recv.at[way, step, e], dp=towards[way]
        )

    def gather_step(buf, own, send, recv, step):
        for e in range(experts):
            for way in (RIGHT, LEFT):
                if step > 0 and gather_has(way, step - 1, e):
                    gather_copy(buf, own, send, recv, way, step - 1, e).wait_recv()
                if gather_has(way, step, e):
                    gather_copy(buf, own, send, recv, way, step, e).start()

    def gather_end(buf, own, send, recv):
        for step in range(half):
            for e in range(experts):
                for way in (RIGHT, LEFT):
                    if gather_has(way, step, e):
                        gather_copy(buf, own, send, recv, way, step, e).wait_send()

    grad_ring = (grad_all, picked_grad, grad_send, grad_recv)
    act_ring = (act_sq, None, act_send, act_recv)
    gather_step(*grad_ring, 0)

    units = {}
    for step in range(half + 1):
        units[step] = []
        for e in range(experts):
            for way in (RIGHT, LEFT) if 0 < step < half else (RIGHT,):
                units[step].append((way, e))
    first = {step: sum(len(units[s]) for s in range(step)) for step in units}

    def unit_rows(step, way):
        return rows(ring_index(place - step if way == RIGHT else place + step, n))

    tile = min(256, columns)

    def project(step):
        for e in range(experts):
            ways = [w for (w, x) in units[step] if x == e]
            at = [first[step] + units[step].index((w, e)) for w in ways]

            @pl.loop(0, columns // tile)
            def _(c):
                cols = pl.ds(pl.multiple_of(c * tile, tile), tile)
                if step == 0:
                    lhs = picked_grad[e]
                else:
                    lhs = jnp.concatenate([grad_all[e, unit_rows(step, w), :] for w in ways], axis=0)
                out = jnp.dot(lhs, grad_w[e, :, cols], preferred_element_type=jnp.float32)
                for i, u in enumerate(at):
                    grad_part[u, :, cols] = out[i * cap : (i + 1) * cap]

        for i in range(len(units[step])):
            u = first[step] + i

            @pl.when(mine != u % m)
            def _():
                part_copy(u).start()

    def part_copy(u):
        q, k = u % m, u // m
        slot = lax.rem(mine - q - 1 + 2 * m, m)
        return remote(
            grad_part.at[u], grad_in.at[k, slot], part_send.at[u], part_recv.at[k, slot], owner=q
        )

    def square_copy(u, step, way, e, j):
        chunk = unit_rows(step, way)
        return remote(
            grad_sq.at[e, chunk, :], grad_sq.at[e, chunk, :],
            sq_send.at[u // m, j - 1], sq_recv.at[u], owner=lax.rem(mine + j, m),
        )

    def reduce(step):
        for i, (way, e) in enumerate(units[step]):
            u = first[step] + i
            q, k = u % m, u // m

            @pl.when(mine == q)
            def _():
                total = grad_part[u]
                for slot in range(m - 1):
                    pltpu.make_async_copy(
                        grad_in.at[k, slot], grad_in.at[k, slot], part_recv.at[k, slot]
                    ).wait()
                    total = total + grad_in[k, slot]
                grad_sq[e, unit_rows(step, way), :] = jnp.square(total).astype(jnp.bfloat16)
                for j in range(1, m):
                    square_copy(u, step, way, e, j).start()

    def sum_has(way, step, e):
        return 0 < step < half or (step == 0 and e % 2 == way)

    def sum_rows(way, step):
        return rows(ring_index(place + (half - step) if way == RIGHT else place - (half - step), n))

    def sum_copy(way, step, e):
        return remote(
            part.at[e, sum_rows(way, step), :], sums.at[way, step, e],
            sum_send.at[way, step, e], sum_recv.at[way, step, e], dp=towards[way],
        )

    def sum_step(step):
        for e in range(experts):
            for way in (RIGHT, LEFT):
                if step > 0 and sum_has(way, step - 1, e):
                    sum_copy(way, step - 1, e).wait_recv()
                    there = sum_rows(way, step)
                    part[e, there, :] = part[e, there, :] + sums[way, step - 1, e]
                if sum_has(way, step, e):
                    sum_copy(way, step, e).start()

    load_grad.wait()
    project(0)

    @pl.loop(1, n)
    def _(k):
        token_copy(k).wait_recv()

    own_rows.wait()

    def share_copy(k):
        return remote(
            rows_in.at[:, my_rows, :], rows_in.at[:, my_rows, :],
            share_send.at[k], share_recv.at[k], owner=share_base + lax.rem(my_share + k, share),
        )

    for k in range(1, share):
        share_copy(k).start()
    if half > 1:
        gather_step(*grad_ring, 1)
    reduce(0)
    for k in range(1, share):
        share_copy(k).wait_recv()
    load_act.wait()
    act_tile = min(256, act_columns)
    for e in range(experts):

        @pl.loop(0, act_columns // act_tile)
        def _(c):
            cols = pl.ds(pl.multiple_of(c * act_tile, act_tile), act_tile)
            lhs = rows_in[:, e * cap : (e + 1) * cap, :].reshape(n * cap, feats)
            part[e, :, cols] = jnp.dot(lhs, act_w[e, :, cols], preferred_element_type=jnp.float32)

    sum_step(0)
    for step in range(1, half):
        project(step)
        sum_step(step)
        gather_step(*grad_ring, step + 1)
        reduce(step)

    for e in range(experts):
        total = part[e, rows(me), :]
        for way in (RIGHT, LEFT):
            if sum_has(way, half - 1, e):
                sum_copy(way, half - 1, e).wait_recv()
                total = total + sums[way, half - 1, e]
        rounded = total.astype(jnp.bfloat16).astype(jnp.float32)
        act_sq[e, rows(me), :] = jnp.square(rounded).astype(jnp.bfloat16)
        for way in (RIGHT, LEFT):
            if gather_has(way, 0, e):
                gather_copy(*act_ring, way, 0, e).start()
    if half == 1:
        gather_step(*grad_ring, 1)
    project(half)
    for step in range(1, half + 1):
        gather_step(*act_ring, step)
        if step == 1:
            reduce(half)

    for step in units:
        for i, (way, e) in enumerate(units[step]):
            u = first[step] + i

            @pl.when(mine == u % m)
            def _():
                for j in range(1, m):
                    square_copy(u, step, way, e, j).wait_send()

            @pl.when(mine != u % m)
            def _():
                part_copy(u).wait_send()
                square_copy(u, step, way, e, 1).wait_recv()

    @pl.loop(1, n)
    def _(k):
        token_copy(k).wait_send()

    for k in range(1, share):
        share_copy(k).wait_send()
    for step in range(half):
        for e in range(experts):
            for way in (RIGHT, LEFT):
                if sum_has(way, step, e):
                    sum_copy(way, step, e).wait_send()
    gather_end(*grad_ring)
    gather_end(*act_ring)


def exchange(picked_act, picked_grad, act_basis, grad_basis):
    n, m = lax.axis_size("dp"), lax.axis_size("owner")
    experts, cap, window = picked_grad.shape
    feats, act_columns = act_basis.shape[1:]
    columns = grad_basis.shape[2]
    half, count = n // 2, n * experts
    share = min(m, experts * cap // 16)
    kept = -(-count // m)
    dma = pltpu.SemaphoreType.DMA
    vmem = pl.BlockSpec(memory_space=pltpu.VMEM)
    flops = 2 * n * cap * experts * (feats * act_columns + window * columns)
    return pl.pallas_call(
        functools.partial(exchange_kernel, n, m, share),
        out_shape=(
            jax.ShapeDtypeStruct((experts, n * cap, act_columns), jnp.bfloat16),
            jax.ShapeDtypeStruct((experts, n * cap, columns), jnp.bfloat16),
        ),
        in_specs=[vmem, vmem, pl.BlockSpec(memory_space=pl.ANY), pl.BlockSpec(memory_space=pl.ANY)],
        out_specs=(vmem, vmem),
        scratch_shapes=[
            pltpu.VMEM(act_basis.shape, jnp.bfloat16),
            pltpu.VMEM(grad_basis.shape, jnp.bfloat16),
            pltpu.VMEM((n, experts * cap, feats), jnp.bfloat16),
            pltpu.VMEM((experts, n * cap, act_columns), jnp.float32),
            pltpu.VMEM((2, half, experts, cap, act_columns), jnp.float32),
            pltpu.VMEM((experts, n * cap, window), jnp.bfloat16),
            pltpu.VMEM((count, cap, columns), jnp.float32),
            pltpu.VMEM((kept, m - 1, cap, columns), jnp.float32),
            dma((3,)),
            dma((n,)),
            dma((n,)),
            dma((share,)),
            dma((share,)),
            dma((2, half, experts)),
            dma((2, half, experts)),
            dma((2, half, experts)),
            dma((2, half, experts)),
            dma((2, half, experts)),
            dma((2, half, experts)),
            dma((count,)),
            dma((kept, m - 1)),
            dma((kept, m - 1)),
            dma((count,)),
        ],
        compiler_params=pltpu.CompilerParams(
            collective_id=0, has_side_effects=True, vmem_limit_bytes=58 * 2**20
        ),
        cost_estimate=pl.CostEstimate(flops=flops, bytes_accessed=20 * 2**20, transcendentals=0),
    )(picked_act.reshape(experts * cap, picked_act.shape[2]), picked_grad, act_basis, grad_basis)


def per_device(tokens, act_basis, grad_basis, grads, expert_ids):
    tok_rows = tokens.shape[0]
    token_total = tok_rows * lax.axis_size("dp")
    picked_act, picked_grad = compact(expert_ids, tokens, grads, tok_rows // 2)
    act_sq, grad_sq = exchange(picked_act, picked_grad, act_basis, grad_basis)
    return (
        jnp.einsum("erk,era->eka", grad_sq, act_sq, preferred_element_type=jnp.float32)
        / token_total
    )


def solution(mesh):
    placed = (
        P("dp", None),
        P(None, "dp", "owner"),
        P(None, "owner", "dp"),
        P(None, "dp", "owner"),
        P("dp", None),
    )
    return jax.shard_map(
        per_device, mesh=mesh, in_specs=placed, out_specs=P(None, "dp", "owner"), check_vma=False
    )
```

```python
import functools

import jax
import jax.numpy as jnp
from jax import lax
from jax.experimental import pallas as pl
from jax.experimental.pallas import tpu as pltpu
from jax.sharding import PartitionSpec as P

MESH = pl.DeviceIdType.MESH
RIGHT, LEFT = 0, 1


def choose(expert_ids, experts, capacity):
    slot_order = jnp.arange(capacity, dtype=jnp.int32)[:, None]
    choosers = []
    for expert in range(experts):
        routed = jnp.any(expert_ids == expert, axis=1)
        slot_index = jnp.cumsum(routed.astype(jnp.int32)) - 1
        chosen = jnp.logical_and(routed[None, :], slot_index[None, :] == slot_order)
        choosers.append(chosen.astype(jnp.bfloat16))
    return jnp.stack(choosers)


def ring_place(index, size):
    return jnp.where(lax.rem(index, 2) == 0, index // 2, size - 1 - index // 2)


def ring_index(place, size):
    place = lax.rem(place + 2 * size, size)
    return jnp.where(place < size // 2, 2 * place, 2 * (size - 1 - place) + 1)


def exchange_kernel(
    n, m, share, chooser, tokens, grads, act_basis, grad_basis, act_sq, grad_sq,
    picked_act, picked_grad, first_out, first_in, act_w, grad_w, rows_in, part, sums, grad_all, grad_part, grad_in,
    load_sem, tok_send, tok_recv, share_send, share_recv, sum_send, sum_recv,
    grad_send, grad_recv, act_send, act_recv, part_send, part_recv, sq_send, sq_recv,
):
    half = n // 2
    experts, cap, _ = picked_grad.shape
    feats = act_basis.shape[1]
    columns = grad_basis.shape[2]
    act_columns = act_basis.shape[2]
    me = lax.axis_index("dp")
    mine = lax.axis_index("owner")
    place = ring_place(me, n)
    towards = (ring_index(place + 1, n), ring_index(place - 1, n))

    def rows(index):
        return pl.ds(pl.multiple_of(index * cap, cap), cap)

    def remote(src, dst, send, recv, **device):
        return pltpu.make_async_remote_copy(
            src_ref=src, dst_ref=dst, send_sem=send, recv_sem=recv,
            device_id=device, device_id_type=MESH,
        )

    load_act = pltpu.make_async_copy(act_basis, act_w, load_sem.at[0])
    load_grad = pltpu.make_async_copy(grad_basis, grad_w, load_sem.at[1])
    load_grad.start()
    load_act.start()

    barrier = pltpu.get_barrier_semaphore()

    @pl.loop(1, n)
    def _(k):
        pl.semaphore_signal(barrier, inc=1, device_id={"dp": lax.rem(me + k, n)}, device_id_type=MESH)

    @pl.loop(1, m)
    def _(k):
        pl.semaphore_signal(barrier, inc=1, device_id={"owner": lax.rem(mine + k, m)}, device_id_type=MESH)

    for e in range(experts):
        for width, source, target in (
            (tokens.shape[1], tokens, picked_act.at[e * cap : (e + 1) * cap]),
            (grads.shape[2], grads.at[e], picked_grad.at[e]),
        ):
            pick_tile = min(512, width)

            @pl.loop(0, width // pick_tile)
            def _(c):
                cols = pl.ds(pl.multiple_of(c * pick_tile, pick_tile), pick_tile)
                target[:, cols] = jnp.dot(
                    chooser[e], source[:, cols], preferred_element_type=jnp.float32
                ).astype(jnp.bfloat16)

    pl.semaphore_wait(barrier, n + m - 2)

    share_rows = experts * cap // share
    my_share = lax.rem(mine, share)
    share_base = mine - my_share
    my_rows = pl.ds(pl.multiple_of(my_share * share_rows, share_rows), share_rows)

    def features(index):
        return pl.ds(pl.multiple_of(index * feats, feats), feats)

    def token_copy(k):
        to = lax.rem(me + k, n)
        return remote(
            picked_act.at[my_rows, features(to)], rows_in.at[me, my_rows, :],
            tok_send.at[k], tok_recv.at[k], dp=to,
        )

    @pl.loop(1, n)
    def _(k):
        token_copy(k).start()

    own_rows = pltpu.make_async_copy(
        picked_act.at[my_rows, features(me)], rows_in.at[me, my_rows, :], load_sem.at[2]
    )
    own_rows.start()

    def gather_has(way, step, e):
        return step < half - 1 or (step == half - 1 and e % 2 == way)

    def gather_copy(buf, own, send, recv, way, step, e):
        chunk = rows(ring_index(place - step if way == RIGHT else place + step, n))
        src = own.at[e] if own is not None and step == 0 else buf.at[e, chunk, :]
        return remote(
            src, buf.at[e, chunk, :], send.at[way, step, e], recv.at[way, step, e], dp=towards[way]
        )

    def gather_step(buf, own, send, recv, step):
        for e in range(experts):
            for way in (RIGHT, LEFT):
                if step > 0 and gather_has(way, step - 1, e):
                    gather_copy(buf, own, send, recv, way, step - 1, e).wait_recv()
                if gather_has(way, step, e):
                    gather_copy(buf, own, send, recv, way, step, e).start()

    def gather_end(buf, own, send, recv):
        for step in range(half):
            for e in range(experts):
                for way in (RIGHT, LEFT):
                    if gather_has(way, step, e):
                        gather_copy(buf, own, send, recv, way, step, e).wait_send()

    grad_ring = (grad_all, picked_grad, grad_send, grad_recv)
    act_ring = (act_sq, None, act_send, act_recv)
    gather_step(*grad_ring, 0)

    units = {}
    for step in range(half + 1):
        units[step] = []
        for e in range(experts):
            for way in (RIGHT, LEFT) if 0 < step < half else (RIGHT,):
                units[step].append((way, e))
    first = {step: sum(len(units[s]) for s in range(step)) for step in units}

    def unit_rows(step, way):
        return rows(ring_index(place - step if way == RIGHT else place + step, n))

    tile = min(256, columns)

    def project(step):
        for e in range(experts):
            ways = [w for (w, x) in units[step] if x == e]
            at = [first[step] + units[step].index((w, e)) for w in ways]

            @pl.loop(0, columns // tile)
            def _(c):
                cols = pl.ds(pl.multiple_of(c * tile, tile), tile)
                if step == 0:
                    lhs = picked_grad[e]
                else:
                    lhs = jnp.concatenate([grad_all[e, unit_rows(step, w), :] for w in ways], axis=0)
                out = jnp.dot(lhs, grad_w[e, :, cols], preferred_element_type=jnp.float32)
                for i, u in enumerate(at):
                    grad_part[u, :, cols] = out[i * cap : (i + 1) * cap]

        for i in range(len(units[step])):
            u = first[step] + i

            @pl.when(mine != u % m)
            def _():
                part_copy(u).start()

    def part_copy(u):
        q, k = u % m, u // m
        slot = lax.rem(mine - q - 1 + 2 * m, m)
        return remote(
            grad_part.at[u], grad_in.at[k, slot], part_send.at[u], part_recv.at[k, slot], owner=q
        )

    def square_copy(u, step, way, e, j):
        chunk = unit_rows(step, way)
        return remote(
            grad_sq.at[e, chunk, :], grad_sq.at[e, chunk, :],
            sq_send.at[u // m, j - 1], sq_recv.at[u], owner=lax.rem(mine + j, m),
        )

    def reduce(step):
        for i, (way, e) in enumerate(units[step]):
            u = first[step] + i
            q, k = u % m, u // m

            @pl.when(mine == q)
            def _():
                total = grad_part[u]
                for slot in range(m - 1):
                    pltpu.make_async_copy(
                        grad_in.at[k, slot], grad_in.at[k, slot], part_recv.at[k, slot]
                    ).wait()
                    total = total + grad_in[k, slot]
                grad_sq[e, unit_rows(step, way), :] = jnp.square(total).astype(jnp.bfloat16)
                for j in range(1, m):
                    square_copy(u, step, way, e, j).start()

    def sum_has(way, step, e):
        return 0 < step < half or (step == 0 and e % 2 == way)

    def sum_rows(way, step):
        return rows(ring_index(place + (half - step) if way == RIGHT else place - (half - step), n))

    def sum_first(way, step, e):
        return step == 0 or (step == 1 and e % 2 != way)

    def sum_copy(way, step, e):
        narrow = sum_first(way, step, e)
        return remote(
            first_out.at[way, e] if narrow else part.at[e, sum_rows(way, step), :],
            first_in.at[way, e] if narrow else sums.at[way, step, e],
            sum_send.at[way, step, e], sum_recv.at[way, step, e], dp=towards[way],
        )

    def sum_arrived(way, step, e):
        if sum_first(way, step, e):
            return first_in[way, e].astype(jnp.float32)
        return sums[way, step, e]

    def sum_step(step):
        for e in range(experts):
            for way in (RIGHT, LEFT):
                if step > 0 and sum_has(way, step - 1, e):
                    sum_copy(way, step - 1, e).wait_recv()
                    there = sum_rows(way, step)
                    part[e, there, :] = part[e, there, :] + sum_arrived(way, step - 1, e)
                if sum_has(way, step, e):
                    if sum_first(way, step, e):
                        first_out[way, e] = part[e, sum_rows(way, step), :].astype(jnp.bfloat16)
                    sum_copy(way, step, e).start()

    load_grad.wait()
    project(0)

    @pl.loop(1, n)
    def _(k):
        token_copy(k).wait_recv()

    own_rows.wait()

    def share_copy(k):
        return remote(
            rows_in.at[:, my_rows, :], rows_in.at[:, my_rows, :],
            share_send.at[k], share_recv.at[k], owner=share_base + lax.rem(my_share + k, share),
        )

    for k in range(1, share):
        share_copy(k).start()
    if half > 1:
        gather_step(*grad_ring, 1)
    reduce(0)
    for k in range(1, share):
        share_copy(k).wait_recv()
    load_act.wait()
    act_tile = min(256, act_columns)
    for e in range(experts):

        @pl.loop(0, act_columns // act_tile)
        def _(c):
            cols = pl.ds(pl.multiple_of(c * act_tile, act_tile), act_tile)
            lhs = rows_in[:, e * cap : (e + 1) * cap, :].reshape(n * cap, feats)
            part[e, :, cols] = jnp.dot(lhs, act_w[e, :, cols], preferred_element_type=jnp.float32)

    sum_step(0)
    for step in range(1, half):
        project(step)
        sum_step(step)
        gather_step(*grad_ring, step + 1)
        reduce(step)

    for e in range(experts):
        total = part[e, rows(me), :]
        for way in (RIGHT, LEFT):
            if sum_has(way, half - 1, e):
                sum_copy(way, half - 1, e).wait_recv()
                total = total + sum_arrived(way, half - 1, e)
        rounded = total.astype(jnp.bfloat16).astype(jnp.float32)
        act_sq[e, rows(me), :] = jnp.square(rounded).astype(jnp.bfloat16)
        for way in (RIGHT, LEFT):
            if gather_has(way, 0, e):
                gather_copy(*act_ring, way, 0, e).start()
    if half == 1:
        gather_step(*grad_ring, 1)
    project(half)
    for step in range(1, half + 1):
        gather_step(*act_ring, step)
        if step == 1:
            reduce(half)

    for step in units:
        for i, (way, e) in enumerate(units[step]):
            u = first[step] + i

            @pl.when(mine == u % m)
            def _():
                for j in range(1, m):
                    square_copy(u, step, way, e, j).wait_send()

            @pl.when(mine != u % m)
            def _():
                part_copy(u).wait_send()
                square_copy(u, step, way, e, 1).wait_recv()

    @pl.loop(1, n)
    def _(k):
        token_copy(k).wait_send()

    for k in range(1, share):
        share_copy(k).wait_send()
    for step in range(half):
        for e in range(experts):
            for way in (RIGHT, LEFT):
                if sum_has(way, step, e):
                    sum_copy(way, step, e).wait_send()
    gather_end(*grad_ring)
    gather_end(*act_ring)


def exchange(chooser, tokens, grads, act_basis, grad_basis):
    n, m = lax.axis_size("dp"), lax.axis_size("owner")
    experts, cap, _ = chooser.shape
    window = grads.shape[2]
    feats, act_columns = act_basis.shape[1:]
    columns = grad_basis.shape[2]
    half, count = n // 2, n * experts
    share = min(m, experts * cap // 16)
    kept = -(-count // m)
    dma = pltpu.SemaphoreType.DMA
    vmem = pl.BlockSpec(memory_space=pltpu.VMEM)
    flops = 2 * n * cap * experts * (feats * act_columns + window * columns)
    return pl.pallas_call(
        functools.partial(exchange_kernel, n, m, share),
        out_shape=(
            jax.ShapeDtypeStruct((experts, n * cap, act_columns), jnp.bfloat16),
            jax.ShapeDtypeStruct((experts, n * cap, columns), jnp.bfloat16),
        ),
        in_specs=[vmem, vmem, vmem, pl.BlockSpec(memory_space=pl.ANY), pl.BlockSpec(memory_space=pl.ANY)],
        out_specs=(vmem, vmem),
        scratch_shapes=[
            pltpu.VMEM((experts * cap, tokens.shape[1]), jnp.bfloat16),
            pltpu.VMEM((experts, cap, window), jnp.bfloat16),
            pltpu.VMEM((2, experts, cap, act_columns), jnp.bfloat16),
            pltpu.VMEM((2, experts, cap, act_columns), jnp.bfloat16),
            pltpu.VMEM(act_basis.shape, jnp.bfloat16),
            pltpu.VMEM(grad_basis.shape, jnp.bfloat16),
            pltpu.VMEM((n, experts * cap, feats), jnp.bfloat16),
            pltpu.VMEM((experts, n * cap, act_columns), jnp.float32),
            pltpu.VMEM((2, half, experts, cap, act_columns), jnp.float32),
            pltpu.VMEM((experts, n * cap, window), jnp.bfloat16),
            pltpu.VMEM((count, cap, columns), jnp.float32),
            pltpu.VMEM((kept, m - 1, cap, columns), jnp.float32),
            dma((3,)),
            dma((n,)),
            dma((n,)),
            dma((share,)),
            dma((share,)),
            dma((2, half, experts)),
            dma((2, half, experts)),
            dma((2, half, experts)),
            dma((2, half, experts)),
            dma((2, half, experts)),
            dma((2, half, experts)),
            dma((count,)),
            dma((kept, m - 1)),
            dma((kept, m - 1)),
            dma((count,)),
        ],
        compiler_params=pltpu.CompilerParams(
            collective_id=0, has_side_effects=True, vmem_limit_bytes=58 * 2**20
        ),
        cost_estimate=pl.CostEstimate(flops=flops, bytes_accessed=20 * 2**20, transcendentals=0),
    )(chooser, tokens, grads, act_basis, grad_basis)


def moment_kernel(token_total, grad_sq, act_sq, out):
    out[0] = (
        lax.dot_general(
            grad_sq[0], act_sq[0], (((0,), (0,)), ((), ())), preferred_element_type=jnp.float32
        )
        / token_total
    )


def moment(grad_sq, act_sq, token_total):
    experts, slots, columns = grad_sq.shape
    act_columns = act_sq.shape[2]
    tile = min(256, columns)
    return pl.pallas_call(
        functools.partial(moment_kernel, token_total),
        out_shape=jax.ShapeDtypeStruct((experts, columns, act_columns), jnp.float32),
        grid=(experts, columns // tile),
        in_specs=[
            pl.BlockSpec((1, slots, tile), lambda e, k: (e, 0, k)),
            pl.BlockSpec((1, slots, act_columns), lambda e, k: (e, 0, 0)),
        ],
        out_specs=pl.BlockSpec((1, tile, act_columns), lambda e, k: (e, k, 0)),
        compiler_params=pltpu.CompilerParams(vmem_limit_bytes=32 * 2**20),
    )(grad_sq, act_sq)


def per_device(tokens, act_basis, grad_basis, grads, expert_ids):
    tok_rows = tokens.shape[0]
    token_total = tok_rows * lax.axis_size("dp")
    chooser = choose(expert_ids, grads.shape[0], tok_rows // 2)
    act_sq, grad_sq = exchange(chooser, tokens, grads, act_basis, grad_basis)
    return moment(grad_sq, act_sq, token_total)


def solution(mesh):
    placed = (
        P("dp", None),
        P(None, "dp", "owner"),
        P(None, "owner", "dp"),
        P(None, "dp", "owner"),
        P("dp", None),
    )
    return jax.shard_map(
        per_device, mesh=mesh, in_specs=placed, out_specs=P(None, "dp", "owner"), check_vma=False
    )
```

```python
import functools

import jax
import jax.numpy as jnp
from jax import lax
from jax.experimental import pallas as pl
from jax.experimental.pallas import tpu as pltpu
from jax.sharding import PartitionSpec as P

MESH = pl.DeviceIdType.MESH
RIGHT, LEFT = 0, 1
KNEE, TOP = 8.0, 32767.0


def encode(value):
    code = TOP * value / (jnp.abs(value) + KNEE)
    return (code + jnp.where(value >= 0, 0.5, -0.5)).astype(jnp.int32).astype(jnp.int16)


def decode(code):
    code = code.astype(jnp.int32).astype(jnp.float32)
    return KNEE * code / (TOP - jnp.abs(code))


def power_scale(norm_sq):
    scale, inverse = jnp.full_like(norm_sq, 0.25), jnp.full_like(norm_sq, 4.0)
    norm_sq = norm_sq * 0.0625
    for k in (16, 8, 4, 2, 1):
        more = norm_sq * 4.0**k < 16384.0
        scale = jnp.where(more, scale * 2.0**k, scale)
        inverse = jnp.where(more, inverse * 0.5**k, inverse)
        norm_sq = jnp.where(more, norm_sq * 4.0**k, norm_sq)
    return scale, inverse


def choose(expert_ids, experts, capacity):
    slot_order = jnp.arange(capacity, dtype=jnp.int32)[:, None]
    choosers = []
    for expert in range(experts):
        routed = jnp.any(expert_ids == expert, axis=1)
        slot_index = jnp.cumsum(routed.astype(jnp.int32)) - 1
        chosen = jnp.logical_and(routed[None, :], slot_index[None, :] == slot_order)
        choosers.append(chosen.astype(jnp.bfloat16))
    return jnp.stack(choosers)


def ring_place(index, size):
    return jnp.where(lax.rem(index, 2) == 0, index // 2, size - 1 - index // 2)


def ring_index(place, size):
    place = lax.rem(place + 2 * size, size)
    return jnp.where(place < size // 2, 2 * place, 2 * (size - 1 - place) + 1)


def exchange_kernel(
    n, m, share, chooser, tokens, grads, act_basis, grad_basis, act_sq, grad_sq,
    picked_act, picked_grad, unscale, sum_out, sum_in, act_w, grad_w, rows_in, part, grad_all, grad_part, grad_in,
    load_sem, tok_send, tok_recv, share_send, share_recv, sum_send, sum_recv,
    grad_send, grad_recv, act_send, act_recv, part_send, part_recv, sq_send, sq_recv,
):
    half = n // 2
    experts, cap, _ = picked_grad.shape
    feats = act_basis.shape[1]
    columns = grad_basis.shape[2]
    act_columns = act_basis.shape[2]
    me = lax.axis_index("dp")
    mine = lax.axis_index("owner")
    place = ring_place(me, n)
    towards = (ring_index(place + 1, n), ring_index(place - 1, n))

    def rows(index):
        return pl.ds(pl.multiple_of(index * cap, cap), cap)

    def remote(src, dst, send, recv, **device):
        return pltpu.make_async_remote_copy(
            src_ref=src, dst_ref=dst, send_sem=send, recv_sem=recv,
            device_id=device, device_id_type=MESH,
        )

    load_act = pltpu.make_async_copy(act_basis, act_w, load_sem.at[0])
    load_grad = pltpu.make_async_copy(grad_basis, grad_w, load_sem.at[1])
    load_grad.start()
    load_act.start()

    barrier = pltpu.get_barrier_semaphore()

    @pl.loop(1, n)
    def _(k):
        pl.semaphore_signal(barrier, inc=1, device_id={"dp": lax.rem(me + k, n)}, device_id_type=MESH)

    @pl.loop(1, m)
    def _(k):
        pl.semaphore_signal(barrier, inc=1, device_id={"owner": lax.rem(mine + k, m)}, device_id_type=MESH)

    for e in range(experts):
        for width, source, target in (
            (tokens.shape[1], tokens, picked_act.at[e * cap : (e + 1) * cap]),
            (grads.shape[2], grads.at[e], picked_grad.at[e]),
        ):
            pick_tile = min(512, width)

            @pl.loop(0, width // pick_tile)
            def _(c):
                cols = pl.ds(pl.multiple_of(c * pick_tile, pick_tile), pick_tile)
                target[:, cols] = jnp.dot(
                    chooser[e], source[:, cols], preferred_element_type=jnp.float32
                ).astype(jnp.bfloat16)

        row = picked_act[e * cap : (e + 1) * cap].astype(jnp.float32)
        scale, inverse = power_scale(jnp.sum(row * row, axis=1, keepdims=True))
        picked_act[e * cap : (e + 1) * cap] = (row * scale).astype(jnp.bfloat16)
        unscale[e] = jnp.broadcast_to(inverse, unscale.shape[1:])

    pl.semaphore_wait(barrier, n + m - 2)

    share_rows = experts * cap // share
    my_share = lax.rem(mine, share)
    share_base = mine - my_share
    my_rows = pl.ds(pl.multiple_of(my_share * share_rows, share_rows), share_rows)

    def features(index):
        return pl.ds(pl.multiple_of(index * feats, feats), feats)

    def token_copy(k):
        to = lax.rem(me + k, n)
        return remote(
            picked_act.at[my_rows, features(to)], rows_in.at[me, my_rows, :],
            tok_send.at[k], tok_recv.at[k], dp=to,
        )

    @pl.loop(1, n)
    def _(k):
        token_copy(k).start()

    own_rows = pltpu.make_async_copy(
        picked_act.at[my_rows, features(me)], rows_in.at[me, my_rows, :], load_sem.at[2]
    )
    own_rows.start()

    def gather_has(way, step, e):
        return step < half - 1 or (step == half - 1 and e % 2 == way)

    def gather_copy(buf, own, send, recv, way, step, e):
        chunk = rows(ring_index(place - step if way == RIGHT else place + step, n))
        src = own.at[e] if own is not None and step == 0 else buf.at[e, chunk, :]
        return remote(
            src, buf.at[e, chunk, :], send.at[way, step, e], recv.at[way, step, e], dp=towards[way]
        )

    def gather_step(buf, own, send, recv, step):
        for e in range(experts):
            for way in (RIGHT, LEFT):
                if step > 0 and gather_has(way, step - 1, e):
                    gather_copy(buf, own, send, recv, way, step - 1, e).wait_recv()
                if gather_has(way, step, e):
                    gather_copy(buf, own, send, recv, way, step, e).start()

    def gather_end(buf, own, send, recv):
        for step in range(half):
            for e in range(experts):
                for way in (RIGHT, LEFT):
                    if gather_has(way, step, e):
                        gather_copy(buf, own, send, recv, way, step, e).wait_send()

    grad_ring = (grad_all, picked_grad, grad_send, grad_recv)
    act_ring = (act_sq, None, act_send, act_recv)
    gather_step(*grad_ring, 0)

    units = {}
    for step in range(half + 1):
        units[step] = []
        for e in range(experts):
            for way in (RIGHT, LEFT) if 0 < step < half else (RIGHT,):
                units[step].append((way, e))
    first = {step: sum(len(units[s]) for s in range(step)) for step in units}

    def unit_rows(step, way):
        return rows(ring_index(place - step if way == RIGHT else place + step, n))

    tile = min(256, columns)

    def project(step):
        for e in range(experts):
            ways = [w for (w, x) in units[step] if x == e]
            at = [first[step] + units[step].index((w, e)) for w in ways]

            @pl.loop(0, columns // tile)
            def _(c):
                cols = pl.ds(pl.multiple_of(c * tile, tile), tile)
                if step == 0:
                    lhs = picked_grad[e]
                else:
                    lhs = jnp.concatenate([grad_all[e, unit_rows(step, w), :] for w in ways], axis=0)
                out = jnp.dot(lhs, grad_w[e, :, cols], preferred_element_type=jnp.float32)
                for i, u in enumerate(at):
                    grad_part[u, :, cols] = out[i * cap : (i + 1) * cap]

        for i in range(len(units[step])):
            u = first[step] + i

            @pl.when(mine != u % m)
            def _():
                part_copy(u).start()

    def part_copy(u):
        q, k = u % m, u // m
        slot = lax.rem(mine - q - 1 + 2 * m, m)
        return remote(
            grad_part.at[u], grad_in.at[k, slot], part_send.at[u], part_recv.at[k, slot], owner=q
        )

    def square_copy(u, step, way, e, j):
        chunk = unit_rows(step, way)
        return remote(
            grad_sq.at[e, chunk, :], grad_sq.at[e, chunk, :],
            sq_send.at[u // m, j - 1], sq_recv.at[u], owner=lax.rem(mine + j, m),
        )

    def reduce(step):
        for i, (way, e) in enumerate(units[step]):
            u = first[step] + i
            q, k = u % m, u // m

            @pl.when(mine == q)
            def _():
                total = grad_part[u]
                for slot in range(m - 1):
                    pltpu.make_async_copy(
                        grad_in.at[k, slot], grad_in.at[k, slot], part_recv.at[k, slot]
                    ).wait()
                    total = total + grad_in[k, slot]
                grad_sq[e, unit_rows(step, way), :] = jnp.square(total).astype(jnp.bfloat16)
                for j in range(1, m):
                    square_copy(u, step, way, e, j).start()

    def sum_has(way, step, e):
        return 0 < step < half or (step == 0 and e % 2 == way)

    def sum_rows(way, step):
        return rows(ring_index(place + (half - step) if way == RIGHT else place - (half - step), n))

    def sum_copy(way, step, e):
        return remote(
            sum_out.at[way, step, e], sum_in.at[way, step, e],
            sum_send.at[way, step, e], sum_recv.at[way, step, e], dp=towards[way],
        )

    def sum_step(step):
        for e in range(experts):
            for way in (RIGHT, LEFT):
                if not sum_has(way, step, e):
                    continue
                total = part[e, sum_rows(way, step), :]
                if step > 0 and sum_has(way, step - 1, e):
                    sum_copy(way, step - 1, e).wait_recv()
                    total = total + decode(sum_in[way, step - 1, e])
                sum_out[way, step, e] = encode(total)
                sum_copy(way, step, e).start()

    load_grad.wait()
    project(0)

    @pl.loop(1, n)
    def _(k):
        token_copy(k).wait_recv()

    own_rows.wait()

    def share_copy(k):
        return remote(
            rows_in.at[:, my_rows, :], rows_in.at[:, my_rows, :],
            share_send.at[k], share_recv.at[k], owner=share_base + lax.rem(my_share + k, share),
        )

    for k in range(1, share):
        share_copy(k).start()
    if half > 1:
        gather_step(*grad_ring, 1)
    reduce(0)
    for k in range(1, share):
        share_copy(k).wait_recv()
    load_act.wait()
    act_tile = min(256, act_columns)
    for e in range(experts):

        @pl.loop(0, act_columns // act_tile)
        def _(c):
            cols = pl.ds(pl.multiple_of(c * act_tile, act_tile), act_tile)
            lhs = rows_in[:, e * cap : (e + 1) * cap, :].reshape(n * cap, feats)
            part[e, :, cols] = jnp.dot(lhs, act_w[e, :, cols], preferred_element_type=jnp.float32)

    sum_step(0)
    for step in range(1, half):
        project(step)
        sum_step(step)
        gather_step(*grad_ring, step + 1)
        reduce(step)

    for e in range(experts):
        total = part[e, rows(me), :]
        for way in (RIGHT, LEFT):
            if sum_has(way, half - 1, e):
                sum_copy(way, half - 1, e).wait_recv()
                total = total + decode(sum_in[way, half - 1, e])
        rounded = (total * unscale[e, :, :1]).astype(jnp.bfloat16).astype(jnp.float32)
        act_sq[e, rows(me), :] = jnp.square(rounded).astype(jnp.bfloat16)
        for way in (RIGHT, LEFT):
            if gather_has(way, 0, e):
                gather_copy(*act_ring, way, 0, e).start()
    if half == 1:
        gather_step(*grad_ring, 1)
    project(half)
    for step in range(1, half + 1):
        gather_step(*act_ring, step)
        if step == 1:
            reduce(half)

    for step in units:
        for i, (way, e) in enumerate(units[step]):
            u = first[step] + i

            @pl.when(mine == u % m)
            def _():
                for j in range(1, m):
                    square_copy(u, step, way, e, j).wait_send()

            @pl.when(mine != u % m)
            def _():
                part_copy(u).wait_send()
                square_copy(u, step, way, e, 1).wait_recv()

    @pl.loop(1, n)
    def _(k):
        token_copy(k).wait_send()

    for k in range(1, share):
        share_copy(k).wait_send()
    for step in range(half):
        for e in range(experts):
            for way in (RIGHT, LEFT):
                if sum_has(way, step, e):
                    sum_copy(way, step, e).wait_send()
    gather_end(*grad_ring)
    gather_end(*act_ring)


def exchange(chooser, tokens, grads, act_basis, grad_basis):
    n, m = lax.axis_size("dp"), lax.axis_size("owner")
    experts, cap, _ = chooser.shape
    window = grads.shape[2]
    feats, act_columns = act_basis.shape[1:]
    columns = grad_basis.shape[2]
    half, count = n // 2, n * experts
    share = min(m, experts * cap // 16)
    kept = -(-count // m)
    dma = pltpu.SemaphoreType.DMA
    vmem = pl.BlockSpec(memory_space=pltpu.VMEM)
    flops = 2 * n * cap * experts * (feats * act_columns + window * columns)
    return pl.pallas_call(
        functools.partial(exchange_kernel, n, m, share),
        out_shape=(
            jax.ShapeDtypeStruct((experts, n * cap, act_columns), jnp.bfloat16),
            jax.ShapeDtypeStruct((experts, n * cap, columns), jnp.bfloat16),
        ),
        in_specs=[vmem, vmem, vmem, pl.BlockSpec(memory_space=pl.ANY), pl.BlockSpec(memory_space=pl.ANY)],
        out_specs=(vmem, vmem),
        scratch_shapes=[
            pltpu.VMEM((experts * cap, tokens.shape[1]), jnp.bfloat16),
            pltpu.VMEM((experts, cap, window), jnp.bfloat16),
            pltpu.VMEM((experts, cap, 128), jnp.float32),
            pltpu.VMEM((2, half, experts, cap, act_columns), jnp.int16),
            pltpu.VMEM((2, half, experts, cap, act_columns), jnp.int16),
            pltpu.VMEM(act_basis.shape, jnp.bfloat16),
            pltpu.VMEM(grad_basis.shape, jnp.bfloat16),
            pltpu.VMEM((n, experts * cap, feats), jnp.bfloat16),
            pltpu.VMEM((experts, n * cap, act_columns), jnp.float32),
            pltpu.VMEM((experts, n * cap, window), jnp.bfloat16),
            pltpu.VMEM((count, cap, columns), jnp.float32),
            pltpu.VMEM((kept, m - 1, cap, columns), jnp.float32),
            dma((3,)),
            dma((n,)),
            dma((n,)),
            dma((share,)),
            dma((share,)),
            dma((2, half, experts)),
            dma((2, half, experts)),
            dma((2, half, experts)),
            dma((2, half, experts)),
            dma((2, half, experts)),
            dma((2, half, experts)),
            dma((count,)),
            dma((kept, m - 1)),
            dma((kept, m - 1)),
            dma((count,)),
        ],
        compiler_params=pltpu.CompilerParams(
            collective_id=0, has_side_effects=True, vmem_limit_bytes=58 * 2**20
        ),
        cost_estimate=pl.CostEstimate(flops=flops, bytes_accessed=20 * 2**20, transcendentals=0),
    )(chooser, tokens, grads, act_basis, grad_basis)


def moment_kernel(token_total, tile, grad_sq, act_sq, out):
    e = pl.program_id(0)
    cols = pl.ds(pl.multiple_of(pl.program_id(1) * tile, tile), tile)
    out[0] = (
        lax.dot_general(
            grad_sq[e, :, cols], act_sq[e], (((0,), (0,)), ((), ())),
            preferred_element_type=jnp.float32,
        )
        / token_total
    )


def moment(grad_sq, act_sq, token_total):
    experts, _, columns = grad_sq.shape
    act_columns = act_sq.shape[2]
    tile = min(256, columns)
    vmem = pl.BlockSpec(memory_space=pltpu.VMEM)
    return pl.pallas_call(
        functools.partial(moment_kernel, token_total, tile),
        out_shape=jax.ShapeDtypeStruct((experts, columns, act_columns), jnp.float32),
        grid=(experts, columns // tile),
        in_specs=[vmem, vmem],
        out_specs=pl.BlockSpec((1, tile, act_columns), lambda e, k: (e, k, 0)),
        compiler_params=pltpu.CompilerParams(vmem_limit_bytes=32 * 2**20),
    )(grad_sq, act_sq)


def per_device(tokens, act_basis, grad_basis, grads, expert_ids):
    tok_rows = tokens.shape[0]
    token_total = tok_rows * lax.axis_size("dp")
    chooser = choose(expert_ids, grads.shape[0], tok_rows // 2)
    act_sq, grad_sq = exchange(chooser, tokens, grads, act_basis, grad_basis)
    return moment(grad_sq, act_sq, token_total)


def solution(mesh):
    placed = (
        P("dp", None),
        P(None, "dp", "owner"),
        P(None, "owner", "dp"),
        P(None, "dp", "owner"),
        P("dp", None),
    )
    return jax.shard_map(
        per_device, mesh=mesh, in_specs=placed, out_specs=P(None, "dp", "owner"), check_vma=False
    )
```

```python
import functools

import jax
import jax.numpy as jnp
from jax import lax
from jax.experimental import pallas as pl
from jax.experimental.pallas import tpu as pltpu
from jax.sharding import PartitionSpec as P

MESH = pl.DeviceIdType.MESH
RIGHT, LEFT = 0, 1
KNEE, TOP = 8.0, 32767.0


def encode(value):
    code = TOP * value / (jnp.abs(value) + KNEE)
    return (code + jnp.where(value >= 0, 0.5, -0.5)).astype(jnp.int32).astype(jnp.int16)


def decode(code):
    code = code.astype(jnp.int32).astype(jnp.float32)
    return KNEE * code / (TOP - jnp.abs(code))


def power_scale(norm_sq):
    scale, inverse = jnp.full_like(norm_sq, 0.25), jnp.full_like(norm_sq, 4.0)
    norm_sq = norm_sq * 0.0625
    for k in (16, 8, 4, 2, 1):
        more = norm_sq * 4.0**k < 16384.0
        scale = jnp.where(more, scale * 2.0**k, scale)
        inverse = jnp.where(more, inverse * 0.5**k, inverse)
        norm_sq = jnp.where(more, norm_sq * 4.0**k, norm_sq)
    return scale, inverse


def choose(expert_ids, experts, capacity):
    slot_order = jnp.arange(capacity, dtype=jnp.int32)[:, None]
    choosers = []
    for expert in range(experts):
        routed = jnp.any(expert_ids == expert, axis=1)
        slot_index = jnp.cumsum(routed.astype(jnp.int32)) - 1
        chosen = jnp.logical_and(routed[None, :], slot_index[None, :] == slot_order)
        choosers.append(chosen.astype(jnp.bfloat16))
    return jnp.stack(choosers)


def ring_place(index, size):
    return jnp.where(lax.rem(index, 2) == 0, index // 2, size - 1 - index // 2)


def ring_index(place, size):
    place = lax.rem(place + 2 * size, size)
    return jnp.where(place < size // 2, 2 * place, 2 * (size - 1 - place) + 1)


def exchange_kernel(
    n, m, share, chooser, tokens, grads, act_basis, grad_basis, act_sq, grad_sq,
    picked_act, picked_grad, unscale, sum_out, sum_in, act_w, grad_w, rows_in, part, grad_all, grad_part, grad_in,
    load_sem, tok_send, tok_recv, share_send, share_recv, sum_send, sum_recv,
    grad_send, grad_recv, act_send, act_recv, part_send, part_recv, sq_send, sq_recv,
):
    half = n // 2
    experts, cap, _ = picked_grad.shape
    feats = act_basis.shape[1]
    columns = grad_basis.shape[2]
    act_columns = act_basis.shape[2]
    me = lax.axis_index("dp")
    mine = lax.axis_index("owner")
    place = ring_place(me, n)
    towards = (ring_index(place + 1, n), ring_index(place - 1, n))

    def rows(index):
        return pl.ds(pl.multiple_of(index * cap, cap), cap)

    def remote(src, dst, send, recv, **device):
        return pltpu.make_async_remote_copy(
            src_ref=src, dst_ref=dst, send_sem=send, recv_sem=recv,
            device_id=device, device_id_type=MESH,
        )

    load_act = pltpu.make_async_copy(act_basis, act_w, load_sem.at[0])
    load_grad = pltpu.make_async_copy(grad_basis, grad_w, load_sem.at[1])
    load_grad.start()
    load_act.start()

    barrier = pltpu.get_barrier_semaphore()

    @pl.loop(1, n)
    def _(k):
        pl.semaphore_signal(barrier, inc=1, device_id={"dp": lax.rem(me + k, n)}, device_id_type=MESH)

    @pl.loop(1, m)
    def _(k):
        pl.semaphore_signal(barrier, inc=1, device_id={"owner": lax.rem(mine + k, m)}, device_id_type=MESH)

    for e in range(experts):
        for width, source, target in (
            (tokens.shape[1], tokens, picked_act.at[e * cap : (e + 1) * cap]),
            (grads.shape[2], grads.at[e], picked_grad.at[e]),
        ):
            pick_tile = min(512, width)

            @pl.loop(0, width // pick_tile)
            def _(c):
                cols = pl.ds(pl.multiple_of(c * pick_tile, pick_tile), pick_tile)
                target[:, cols] = jnp.dot(
                    chooser[e], source[:, cols], preferred_element_type=jnp.float32
                ).astype(jnp.bfloat16)

        row = picked_act[e * cap : (e + 1) * cap].astype(jnp.float32)
        scale, inverse = power_scale(jnp.sum(row * row, axis=1, keepdims=True))
        picked_act[e * cap : (e + 1) * cap] = (row * scale).astype(jnp.bfloat16)
        unscale[e] = jnp.broadcast_to(inverse, unscale.shape[1:])

    pl.semaphore_wait(barrier, n + m - 2)

    share_rows = experts * cap // share
    my_share = lax.rem(mine, share)
    share_base = mine - my_share
    my_rows = pl.ds(pl.multiple_of(my_share * share_rows, share_rows), share_rows)

    def features(index):
        return pl.ds(pl.multiple_of(index * feats, feats), feats)

    def token_copy(k):
        to = lax.rem(me + k, n)
        return remote(
            picked_act.at[my_rows, features(to)], rows_in.at[me, my_rows, :],
            tok_send.at[k], tok_recv.at[k], dp=to,
        )

    @pl.loop(1, n)
    def _(k):
        token_copy(k).start()

    own_rows = pltpu.make_async_copy(
        picked_act.at[my_rows, features(me)], rows_in.at[me, my_rows, :], load_sem.at[2]
    )
    own_rows.start()

    def gather_has(way, step, e):
        return step < half - 1 or (step == half - 1 and e % 2 == way)

    def gather_copy(buf, own, send, recv, way, step, e):
        chunk = rows(ring_index(place - step if way == RIGHT else place + step, n))
        src = own.at[e] if own is not None and step == 0 else buf.at[e, chunk, :]
        return remote(
            src, buf.at[e, chunk, :], send.at[way, step, e], recv.at[way, step, e], dp=towards[way]
        )

    def gather_step(buf, own, send, recv, step):
        for e in range(experts):
            for way in (RIGHT, LEFT):
                if step > 0 and gather_has(way, step - 1, e):
                    gather_copy(buf, own, send, recv, way, step - 1, e).wait_recv()
                if gather_has(way, step, e):
                    gather_copy(buf, own, send, recv, way, step, e).start()

    def gather_end(buf, own, send, recv):
        for step in range(half):
            for e in range(experts):
                for way in (RIGHT, LEFT):
                    if gather_has(way, step, e):
                        gather_copy(buf, own, send, recv, way, step, e).wait_send()

    grad_ring = (grad_all, picked_grad, grad_send, grad_recv)
    act_ring = (act_sq, None, act_send, act_recv)
    units = {}
    for step in range(half + 1):
        units[step] = []
        for e in range(experts):
            for way in (RIGHT, LEFT) if 0 < step < half else (RIGHT,):
                units[step].append((way, e))
    first = {step: sum(len(units[s]) for s in range(step)) for step in units}

    def unit_rows(step, way):
        return rows(ring_index(place - step if way == RIGHT else place + step, n))

    tile = min(256, columns)

    def project(step):
        for e in range(experts):
            ways = [w for (w, x) in units[step] if x == e]
            at = [first[step] + units[step].index((w, e)) for w in ways]

            @pl.loop(0, columns // tile)
            def _(c):
                cols = pl.ds(pl.multiple_of(c * tile, tile), tile)
                if step == 0:
                    lhs = picked_grad[e]
                else:
                    lhs = jnp.concatenate([grad_all[e, unit_rows(step, w), :] for w in ways], axis=0)
                out = jnp.dot(lhs, grad_w[e, :, cols], preferred_element_type=jnp.float32)
                for i, u in enumerate(at):
                    grad_part[u, :, cols] = out[i * cap : (i + 1) * cap]

        for i in range(len(units[step])):
            u = first[step] + i

            @pl.when(mine != u % m)
            def _():
                part_copy(u).start()

    def part_copy(u):
        q, k = u % m, u // m
        slot = lax.rem(mine - q - 1 + 2 * m, m)
        return remote(
            grad_part.at[u], grad_in.at[k, slot], part_send.at[u], part_recv.at[k, slot], owner=q
        )

    def square_copy(u, step, way, e, j):
        chunk = unit_rows(step, way)
        return remote(
            grad_sq.at[e, chunk, :], grad_sq.at[e, chunk, :],
            sq_send.at[u // m, j - 1], sq_recv.at[u], owner=lax.rem(mine + j, m),
        )

    def reduce(step):
        for i, (way, e) in enumerate(units[step]):
            u = first[step] + i
            q, k = u % m, u // m

            @pl.when(mine == q)
            def _():
                total = grad_part[u]
                for slot in range(m - 1):
                    pltpu.make_async_copy(
                        grad_in.at[k, slot], grad_in.at[k, slot], part_recv.at[k, slot]
                    ).wait()
                    total = total + grad_in[k, slot]
                grad_sq[e, unit_rows(step, way), :] = jnp.square(total).astype(jnp.bfloat16)
                for j in range(1, m):
                    square_copy(u, step, way, e, j).start()

    def sum_has(way, step, e):
        return 0 < step < half or (step == 0 and e % 2 == way)

    def sum_rows(way, step):
        return rows(ring_index(place + (half - step) if way == RIGHT else place - (half - step), n))

    def sum_copy(way, step, e):
        return remote(
            sum_out.at[way, step, e], sum_in.at[way, step, e],
            sum_send.at[way, step, e], sum_recv.at[way, step, e], dp=towards[way],
        )

    def sum_step(step):
        for e in range(experts):
            for way in (RIGHT, LEFT):
                if not sum_has(way, step, e):
                    continue
                total = part[e, sum_rows(way, step), :]
                if step > 0 and sum_has(way, step - 1, e):
                    sum_copy(way, step - 1, e).wait_recv()
                    total = total + decode(sum_in[way, step - 1, e])
                sum_out[way, step, e] = encode(total)
                sum_copy(way, step, e).start()

    @pl.loop(1, n)
    def _(k):
        token_copy(k).wait_recv()

    own_rows.wait()

    chips = share // 2
    core = lax.rem(my_share, 2)
    chip = my_share // 2

    def share_slice(k):
        start = (core + 2 * lax.rem(chip - k + chips, chips)) * share_rows
        return rows_in.at[:, pl.ds(pl.multiple_of(start, share_rows), share_rows), :]

    def share_copy(k):
        to = share_base + core + 2 * lax.rem(chip + k, chips)
        return remote(share_slice(0), share_slice(0), share_send.at[k], share_recv.at[k], owner=to)

    def pair_copy(k):
        to = share_base + 2 * chip + 1 - core
        at = chips + k
        return remote(share_slice(k), share_slice(k), share_send.at[at], share_recv.at[at], owner=to)

    for k in range(1, chips):
        share_copy(k).start()
    pair_copy(0).start()
    gather_step(*grad_ring, 0)
    load_grad.wait()
    project(0)
    for k in range(1, chips):
        share_copy(k).wait_recv()
        pair_copy(k).start()
    load_act.wait()
    for k in range(chips):
        pair_copy(k).wait_recv()
    act_tile = min(256, act_columns)
    for e in range(experts):

        @pl.loop(0, act_columns // act_tile)
        def _(c):
            cols = pl.ds(pl.multiple_of(c * act_tile, act_tile), act_tile)
            lhs = rows_in[:, e * cap : (e + 1) * cap, :].reshape(n * cap, feats)
            part[e, :, cols] = jnp.dot(lhs, act_w[e, :, cols], preferred_element_type=jnp.float32)

    def act_start():
        for e in range(experts):
            total = part[e, rows(me), :]
            for way in (RIGHT, LEFT):
                if sum_has(way, half - 1, e):
                    sum_copy(way, half - 1, e).wait_recv()
                    total = total + decode(sum_in[way, half - 1, e])
            rounded = (total * unscale[e, :, :1]).astype(jnp.bfloat16).astype(jnp.float32)
            act_sq[e, rows(me), :] = jnp.square(rounded).astype(jnp.bfloat16)
            for way in (RIGHT, LEFT):
                if gather_has(way, 0, e):
                    gather_copy(*act_ring, way, 0, e).start()

    sum_step(0)
    done = 0
    for hop in range(1, 2 * half + 1):
        if hop < half:
            sum_step(hop)
        elif hop == half:
            act_start()
        else:
            gather_step(*act_ring, hop - half)
        while done < min(half, (2 * hop + 1) // 3):
            done += 1
            gather_step(*grad_ring, done)
            project(done)
            reduce(done - 1)
        if hop == 2 * half - 1:
            reduce(half)

    for step in units:
        for i, (way, e) in enumerate(units[step]):
            u = first[step] + i

            @pl.when(mine == u % m)
            def _():
                for j in range(1, m):
                    square_copy(u, step, way, e, j).wait_send()

            @pl.when(mine != u % m)
            def _():
                part_copy(u).wait_send()
                square_copy(u, step, way, e, 1).wait_recv()

    @pl.loop(1, n)
    def _(k):
        token_copy(k).wait_send()

    for k in range(1, chips):
        share_copy(k).wait_send()
    for k in range(chips):
        pair_copy(k).wait_send()
    for step in range(half):
        for e in range(experts):
            for way in (RIGHT, LEFT):
                if sum_has(way, step, e):
                    sum_copy(way, step, e).wait_send()
    gather_end(*grad_ring)
    gather_end(*act_ring)


def exchange(chooser, tokens, grads, act_basis, grad_basis):
    n, m = lax.axis_size("dp"), lax.axis_size("owner")
    experts, cap, _ = chooser.shape
    window = grads.shape[2]
    feats, act_columns = act_basis.shape[1:]
    columns = grad_basis.shape[2]
    half, count = n // 2, n * experts
    share = min(m, experts * cap // 16)
    kept = -(-count // m)
    dma = pltpu.SemaphoreType.DMA
    vmem = pl.BlockSpec(memory_space=pltpu.VMEM)
    flops = 2 * n * cap * experts * (feats * act_columns + window * columns)
    return pl.pallas_call(
        functools.partial(exchange_kernel, n, m, share),
        out_shape=(
            jax.ShapeDtypeStruct((experts, n * cap, act_columns), jnp.bfloat16),
            jax.ShapeDtypeStruct((experts, n * cap, columns), jnp.bfloat16),
        ),
        in_specs=[vmem, vmem, vmem, pl.BlockSpec(memory_space=pl.ANY), pl.BlockSpec(memory_space=pl.ANY)],
        out_specs=(vmem, vmem),
        scratch_shapes=[
            pltpu.VMEM((experts * cap, tokens.shape[1]), jnp.bfloat16),
            pltpu.VMEM((experts, cap, window), jnp.bfloat16),
            pltpu.VMEM((experts, cap, 128), jnp.float32),
            pltpu.VMEM((2, half, experts, cap, act_columns), jnp.int16),
            pltpu.VMEM((2, half, experts, cap, act_columns), jnp.int16),
            pltpu.VMEM(act_basis.shape, jnp.bfloat16),
            pltpu.VMEM(grad_basis.shape, jnp.bfloat16),
            pltpu.VMEM((n, experts * cap, feats), jnp.bfloat16),
            pltpu.VMEM((experts, n * cap, act_columns), jnp.float32),
            pltpu.VMEM((experts, n * cap, window), jnp.bfloat16),
            pltpu.VMEM((count, cap, columns), jnp.float32),
            pltpu.VMEM((kept, m - 1, cap, columns), jnp.float32),
            dma((3,)),
            dma((n,)),
            dma((n,)),
            dma((share,)),
            dma((share,)),
            dma((2, half, experts)),
            dma((2, half, experts)),
            dma((2, half, experts)),
            dma((2, half, experts)),
            dma((2, half, experts)),
            dma((2, half, experts)),
            dma((count,)),
            dma((kept, m - 1)),
            dma((kept, m - 1)),
            dma((count,)),
        ],
        compiler_params=pltpu.CompilerParams(
            collective_id=0, has_side_effects=True, vmem_limit_bytes=58 * 2**20
        ),
        cost_estimate=pl.CostEstimate(flops=flops, bytes_accessed=20 * 2**20, transcendentals=0),
    )(chooser, tokens, grads, act_basis, grad_basis)


def moment_kernel(token_total, tile, grad_sq, act_sq, out):
    e = pl.program_id(0)
    cols = pl.ds(pl.multiple_of(pl.program_id(1) * tile, tile), tile)
    out[0] = (
        lax.dot_general(
            grad_sq[e, :, cols], act_sq[e], (((0,), (0,)), ((), ())),
            preferred_element_type=jnp.float32,
        )
        / token_total
    )


def moment(grad_sq, act_sq, token_total):
    experts, _, columns = grad_sq.shape
    act_columns = act_sq.shape[2]
    tile = min(256, columns)
    vmem = pl.BlockSpec(memory_space=pltpu.VMEM)
    return pl.pallas_call(
        functools.partial(moment_kernel, token_total, tile),
        out_shape=jax.ShapeDtypeStruct((experts, columns, act_columns), jnp.float32),
        grid=(experts, columns // tile),
        in_specs=[vmem, vmem],
        out_specs=pl.BlockSpec((1, tile, act_columns), lambda e, k: (e, k, 0)),
        compiler_params=pltpu.CompilerParams(vmem_limit_bytes=32 * 2**20),
    )(grad_sq, act_sq)


def per_device(tokens, act_basis, grad_basis, grads, expert_ids):
    tok_rows = tokens.shape[0]
    token_total = tok_rows * lax.axis_size("dp")
    chooser = choose(expert_ids, grads.shape[0], tok_rows // 2)
    act_sq, grad_sq = exchange(chooser, tokens, grads, act_basis, grad_basis)
    return moment(grad_sq, act_sq, token_total)


def solution(mesh):
    placed = (
        P("dp", None),
        P(None, "dp", "owner"),
        P(None, "owner", "dp"),
        P(None, "dp", "owner"),
        P("dp", None),
    )
    return jax.shard_map(
        per_device, mesh=mesh, in_specs=placed, out_specs=P(None, "dp", "owner"), check_vma=False
    )
```

```python
import functools

import jax
import jax.numpy as jnp
from jax import lax
from jax.experimental import pallas as pl
from jax.experimental.pallas import tpu as pltpu
from jax.sharding import PartitionSpec as P

MESH = pl.DeviceIdType.MESH
RIGHT, LEFT = 0, 1
KNEE, TOP = 8.0, 32767.0


def encode(value):
    code = TOP * value / (jnp.abs(value) + KNEE)
    return (code + jnp.where(value >= 0, 0.5, -0.5)).astype(jnp.int32).astype(jnp.int16)


def decode(code):
    code = code.astype(jnp.int32).astype(jnp.float32)
    return KNEE * code / (TOP - jnp.abs(code))


def power_scale(norm_sq):
    scale, inverse = jnp.full_like(norm_sq, 0.25), jnp.full_like(norm_sq, 4.0)
    norm_sq = norm_sq * 0.0625
    for k in (16, 8, 4, 2, 1):
        more = norm_sq * 4.0**k < 16384.0
        scale = jnp.where(more, scale * 2.0**k, scale)
        inverse = jnp.where(more, inverse * 0.5**k, inverse)
        norm_sq = jnp.where(more, norm_sq * 4.0**k, norm_sq)
    return scale, inverse


def choose(expert_ids, experts, capacity):
    slot_order = jnp.arange(capacity, dtype=jnp.int32)[:, None]
    choosers = []
    for expert in range(experts):
        routed = jnp.any(expert_ids == expert, axis=1)
        slot_index = jnp.cumsum(routed.astype(jnp.int32)) - 1
        chosen = jnp.logical_and(routed[None, :], slot_index[None, :] == slot_order)
        choosers.append(chosen.astype(jnp.bfloat16))
    return jnp.stack(choosers)


def ring_place(index, size):
    return jnp.where(lax.rem(index, 2) == 0, index // 2, size - 1 - index // 2)


def ring_index(place, size):
    place = lax.rem(place + 2 * size, size)
    return jnp.where(place < size // 2, 2 * place, 2 * (size - 1 - place) + 1)


def exchange_kernel(
    n, m, share, chooser, tokens, grads, act_basis, grad_basis, act_sq, grad_sq,
    picked_act, picked_grad, unscale, sum_out, sum_in, act_w, grad_w, rows_in, part, grad_all, grad_part, grad_out, grad_in,
    load_sem, tok_send, tok_recv, share_send, share_recv, sum_send, sum_recv,
    grad_send, grad_recv, act_send, act_recv, part_send, part_recv, sq_send, sq_recv,
):
    half = n // 2
    experts, cap, _ = picked_grad.shape
    feats = act_basis.shape[1]
    columns = grad_basis.shape[2]
    act_columns = act_basis.shape[2]
    me = lax.axis_index("dp")
    mine = lax.axis_index("owner")
    place = ring_place(me, n)
    towards = (ring_index(place + 1, n), ring_index(place - 1, n))

    def rows(index):
        return pl.ds(pl.multiple_of(index * cap, cap), cap)

    def remote(src, dst, send, recv, **device):
        return pltpu.make_async_remote_copy(
            src_ref=src, dst_ref=dst, send_sem=send, recv_sem=recv,
            device_id=device, device_id_type=MESH,
        )

    load_act = pltpu.make_async_copy(act_basis, act_w, load_sem.at[0])
    load_grad = pltpu.make_async_copy(grad_basis, grad_w, load_sem.at[1])
    load_grad.start()
    load_act.start()

    barrier = pltpu.get_barrier_semaphore()

    @pl.loop(1, n)
    def _(k):
        pl.semaphore_signal(barrier, inc=1, device_id={"dp": lax.rem(me + k, n)}, device_id_type=MESH)

    @pl.loop(1, m)
    def _(k):
        pl.semaphore_signal(barrier, inc=1, device_id={"owner": lax.rem(mine + k, m)}, device_id_type=MESH)

    for e in range(experts):
        for width, source, target in (
            (tokens.shape[1], tokens, picked_act.at[e * cap : (e + 1) * cap]),
            (grads.shape[2], grads.at[e], picked_grad.at[e]),
        ):
            pick_tile = min(512, width)

            @pl.loop(0, width // pick_tile)
            def _(c):
                cols = pl.ds(pl.multiple_of(c * pick_tile, pick_tile), pick_tile)
                target[:, cols] = jnp.dot(
                    chooser[e], source[:, cols], preferred_element_type=jnp.float32
                ).astype(jnp.bfloat16)

        row = picked_act[e * cap : (e + 1) * cap].astype(jnp.float32)
        scale, inverse = power_scale(jnp.sum(row * row, axis=1, keepdims=True))
        picked_act[e * cap : (e + 1) * cap] = (row * scale).astype(jnp.bfloat16)
        unscale[e] = jnp.broadcast_to(inverse, unscale.shape[1:])

    pl.semaphore_wait(barrier, n + m - 2)

    share_rows = experts * cap // share
    my_share = lax.rem(mine, share)
    share_base = mine - my_share
    my_rows = pl.ds(pl.multiple_of(my_share * share_rows, share_rows), share_rows)

    def features(index):
        return pl.ds(pl.multiple_of(index * feats, feats), feats)

    def token_copy(k):
        to = lax.rem(me + k, n)
        return remote(
            picked_act.at[my_rows, features(to)], rows_in.at[me, my_rows, :],
            tok_send.at[k], tok_recv.at[k], dp=to,
        )

    @pl.loop(1, n)
    def _(k):
        token_copy(k).start()

    own_rows = pltpu.make_async_copy(
        picked_act.at[my_rows, features(me)], rows_in.at[me, my_rows, :], load_sem.at[2]
    )
    own_rows.start()

    def gather_has(way, step, e):
        return step < half - 1 or (step == half - 1 and e % 2 == way)

    def gather_copy(buf, own, send, recv, way, step, e):
        chunk = rows(ring_index(place - step if way == RIGHT else place + step, n))
        src = own.at[e] if own is not None and step == 0 else buf.at[e, chunk, :]
        return remote(
            src, buf.at[e, chunk, :], send.at[way, step, e], recv.at[way, step, e], dp=towards[way]
        )

    def gather_step(buf, own, send, recv, step):
        for e in range(experts):
            for way in (RIGHT, LEFT):
                if step > 0 and gather_has(way, step - 1, e):
                    gather_copy(buf, own, send, recv, way, step - 1, e).wait_recv()
                if gather_has(way, step, e):
                    gather_copy(buf, own, send, recv, way, step, e).start()

    def gather_end(buf, own, send, recv):
        for step in range(half):
            for e in range(experts):
                for way in (RIGHT, LEFT):
                    if gather_has(way, step, e):
                        gather_copy(buf, own, send, recv, way, step, e).wait_send()

    grad_ring = (grad_all, picked_grad, grad_send, grad_recv)
    act_ring = (act_sq, None, act_send, act_recv)
    units = {}
    for step in range(half + 1):
        units[step] = []
        for e in range(experts):
            for way in (RIGHT, LEFT) if 0 < step < half else (RIGHT,):
                units[step].append((way, e))
    first = {step: sum(len(units[s]) for s in range(step)) for step in units}

    def unit_rows(step, way):
        return rows(ring_index(place - step if way == RIGHT else place + step, n))

    tile = min(256, columns)

    def project(step):
        for e in range(experts):
            ways = [w for (w, x) in units[step] if x == e]
            at = [first[step] + units[step].index((w, e)) for w in ways]

            @pl.loop(0, columns // tile)
            def _(c):
                cols = pl.ds(pl.multiple_of(c * tile, tile), tile)
                if step == 0:
                    lhs = picked_grad[e]
                else:
                    lhs = jnp.concatenate([grad_all[e, unit_rows(step, w), :] for w in ways], axis=0)
                out = jnp.dot(lhs, grad_w[e, :, cols], preferred_element_type=jnp.float32)
                for i, u in enumerate(at):
                    grad_part[u, :, cols] = out[i * cap : (i + 1) * cap]
                    grad_out[u, :, cols] = out[i * cap : (i + 1) * cap].astype(jnp.bfloat16)

        for i in range(len(units[step])):
            u = first[step] + i

            @pl.when(mine != u % m)
            def _():
                part_copy(u).start()

    def part_copy(u):
        q, k = u % m, u // m
        slot = lax.rem(mine - q - 1 + 2 * m, m)
        return remote(
            grad_out.at[u], grad_in.at[k, slot], part_send.at[u], part_recv.at[k, slot], owner=q
        )

    def square_copy(u, step, way, e, j):
        chunk = unit_rows(step, way)
        return remote(
            grad_sq.at[e, chunk, :], grad_sq.at[e, chunk, :],
            sq_send.at[u // m, j - 1], sq_recv.at[u], owner=lax.rem(mine + j, m),
        )

    def reduce(step):
        for i, (way, e) in enumerate(units[step]):
            u = first[step] + i
            q, k = u % m, u // m

            @pl.when(mine == q)
            def _():
                total = grad_part[u]
                for slot in range(m - 1):
                    pltpu.make_async_copy(
                        grad_in.at[k, slot], grad_in.at[k, slot], part_recv.at[k, slot]
                    ).wait()
                    total = total + grad_in[k, slot].astype(jnp.float32)
                grad_sq[e, unit_rows(step, way), :] = jnp.square(total).astype(jnp.bfloat16)
                for j in range(1, m):
                    square_copy(u, step, way, e, j).start()

    def sum_has(way, step, e):
        return 0 < step < half or (step == 0 and e % 2 == way)

    def sum_rows(way, step):
        return rows(ring_index(place + (half - step) if way == RIGHT else place - (half - step), n))

    def sum_copy(way, step, e):
        return remote(
            sum_out.at[way, step, e], sum_in.at[way, step, e],
            sum_send.at[way, step, e], sum_recv.at[way, step, e], dp=towards[way],
        )

    def sum_step(step):
        for e in range(experts):
            for way in (RIGHT, LEFT):
                if not sum_has(way, step, e):
                    continue
                total = part[e, sum_rows(way, step), :]
                if step > 0 and sum_has(way, step - 1, e):
                    sum_copy(way, step - 1, e).wait_recv()
                    total = total + decode(sum_in[way, step - 1, e])
                sum_out[way, step, e] = encode(total)
                sum_copy(way, step, e).start()

    @pl.loop(1, n)
    def _(k):
        token_copy(k).wait_recv()

    own_rows.wait()

    chips = share // 2
    core = lax.rem(my_share, 2)
    chip = my_share // 2

    def share_slice(k):
        start = (core + 2 * lax.rem(chip - k + chips, chips)) * share_rows
        return rows_in.at[:, pl.ds(pl.multiple_of(start, share_rows), share_rows), :]

    def share_copy(k):
        to = share_base + core + 2 * lax.rem(chip + k, chips)
        return remote(share_slice(0), share_slice(0), share_send.at[k], share_recv.at[k], owner=to)

    def pair_copy(k):
        to = share_base + 2 * chip + 1 - core
        at = chips + k
        return remote(share_slice(k), share_slice(k), share_send.at[at], share_recv.at[at], owner=to)

    for k in range(1, chips):
        share_copy(k).start()
    pair_copy(0).start()
    gather_step(*grad_ring, 0)
    load_grad.wait()
    project(0)
    for k in range(1, chips):
        share_copy(k).wait_recv()
        pair_copy(k).start()
    load_act.wait()
    for k in range(chips):
        pair_copy(k).wait_recv()
    act_tile = min(256, act_columns)
    for e in range(experts):

        @pl.loop(0, act_columns // act_tile)
        def _(c):
            cols = pl.ds(pl.multiple_of(c * act_tile, act_tile), act_tile)
            lhs = rows_in[:, e * cap : (e + 1) * cap, :].reshape(n * cap, feats)
            part[e, :, cols] = jnp.dot(lhs, act_w[e, :, cols], preferred_element_type=jnp.float32)

    def act_start():
        for e in range(experts):
            total = part[e, rows(me), :]
            for way in (RIGHT, LEFT):
                if sum_has(way, half - 1, e):
                    sum_copy(way, half - 1, e).wait_recv()
                    total = total + decode(sum_in[way, half - 1, e])
            rounded = (total * unscale[e, :, :1]).astype(jnp.bfloat16).astype(jnp.float32)
            act_sq[e, rows(me), :] = jnp.square(rounded).astype(jnp.bfloat16)
            for way in (RIGHT, LEFT):
                if gather_has(way, 0, e):
                    gather_copy(*act_ring, way, 0, e).start()

    sum_step(0)
    done = 0
    for hop in range(1, 2 * half + 1):
        if hop < half:
            sum_step(hop)
        elif hop == half:
            act_start()
        else:
            gather_step(*act_ring, hop - half)
        while done < min(half, hop):
            done += 1
            gather_step(*grad_ring, done)
            project(done)
            reduce(done - 1)
        if hop == min(half + 2, 2 * half - 1):
            reduce(half)

    for step in units:
        for i, (way, e) in enumerate(units[step]):
            u = first[step] + i

            @pl.when(mine == u % m)
            def _():
                for j in range(1, m):
                    square_copy(u, step, way, e, j).wait_send()

            @pl.when(mine != u % m)
            def _():
                part_copy(u).wait_send()
                square_copy(u, step, way, e, 1).wait_recv()

    @pl.loop(1, n)
    def _(k):
        token_copy(k).wait_send()

    for k in range(1, chips):
        share_copy(k).wait_send()
    for k in range(chips):
        pair_copy(k).wait_send()
    for step in range(half):
        for e in range(experts):
            for way in (RIGHT, LEFT):
                if sum_has(way, step, e):
                    sum_copy(way, step, e).wait_send()
    gather_end(*grad_ring)
    gather_end(*act_ring)


def exchange(chooser, tokens, grads, act_basis, grad_basis):
    n, m = lax.axis_size("dp"), lax.axis_size("owner")
    experts, cap, _ = chooser.shape
    window = grads.shape[2]
    feats, act_columns = act_basis.shape[1:]
    columns = grad_basis.shape[2]
    half, count = n // 2, n * experts
    share = min(m, experts * cap // 16)
    kept = -(-count // m)
    dma = pltpu.SemaphoreType.DMA
    vmem = pl.BlockSpec(memory_space=pltpu.VMEM)
    flops = 2 * n * cap * experts * (feats * act_columns + window * columns)
    return pl.pallas_call(
        functools.partial(exchange_kernel, n, m, share),
        out_shape=(
            jax.ShapeDtypeStruct((experts, n * cap, act_columns), jnp.bfloat16),
            jax.ShapeDtypeStruct((experts, n * cap, columns), jnp.bfloat16),
        ),
        in_specs=[vmem, vmem, vmem, pl.BlockSpec(memory_space=pl.ANY), pl.BlockSpec(memory_space=pl.ANY)],
        out_specs=(vmem, vmem),
        scratch_shapes=[
            pltpu.VMEM((experts * cap, tokens.shape[1]), jnp.bfloat16),
            pltpu.VMEM((experts, cap, window), jnp.bfloat16),
            pltpu.VMEM((experts, cap, 128), jnp.float32),
            pltpu.VMEM((2, half, experts, cap, act_columns), jnp.int16),
            pltpu.VMEM((2, half, experts, cap, act_columns), jnp.int16),
            pltpu.VMEM(act_basis.shape, jnp.bfloat16),
            pltpu.VMEM(grad_basis.shape, jnp.bfloat16),
            pltpu.VMEM((n, experts * cap, feats), jnp.bfloat16),
            pltpu.VMEM((experts, n * cap, act_columns), jnp.float32),
            pltpu.VMEM((experts, n * cap, window), jnp.bfloat16),
            pltpu.VMEM((count, cap, columns), jnp.float32),
            pltpu.VMEM((count, cap, columns), jnp.bfloat16),
            pltpu.VMEM((kept, m - 1, cap, columns), jnp.bfloat16),
            dma((3,)),
            dma((n,)),
            dma((n,)),
            dma((share,)),
            dma((share,)),
            dma((2, half, experts)),
            dma((2, half, experts)),
            dma((2, half, experts)),
            dma((2, half, experts)),
            dma((2, half, experts)),
            dma((2, half, experts)),
            dma((count,)),
            dma((kept, m - 1)),
            dma((kept, m - 1)),
            dma((count,)),
        ],
        compiler_params=pltpu.CompilerParams(
            collective_id=0, has_side_effects=True, vmem_limit_bytes=58 * 2**20
        ),
        cost_estimate=pl.CostEstimate(flops=flops, bytes_accessed=20 * 2**20, transcendentals=0),
    )(chooser, tokens, grads, act_basis, grad_basis)


def moment_kernel(token_total, tile, grad_sq, act_sq, out):
    e = pl.program_id(0)
    cols = pl.ds(pl.multiple_of(pl.program_id(1) * tile, tile), tile)
    out[0] = (
        lax.dot_general(
            grad_sq[e, :, cols], act_sq[e], (((0,), (0,)), ((), ())),
            preferred_element_type=jnp.float32,
        )
        / token_total
    )


def moment(grad_sq, act_sq, token_total):
    experts, _, columns = grad_sq.shape
    act_columns = act_sq.shape[2]
    tile = min(256, columns)
    vmem = pl.BlockSpec(memory_space=pltpu.VMEM)
    return pl.pallas_call(
        functools.partial(moment_kernel, token_total, tile),
        out_shape=jax.ShapeDtypeStruct((experts, columns, act_columns), jnp.float32),
        grid=(experts, columns // tile),
        in_specs=[vmem, vmem],
        out_specs=pl.BlockSpec((1, tile, act_columns), lambda e, k: (e, k, 0)),
        compiler_params=pltpu.CompilerParams(vmem_limit_bytes=32 * 2**20),
    )(grad_sq, act_sq)


def per_device(tokens, act_basis, grad_basis, grads, expert_ids):
    tok_rows = tokens.shape[0]
    token_total = tok_rows * lax.axis_size("dp")
    chooser = choose(expert_ids, grads.shape[0], tok_rows // 2)
    act_sq, grad_sq = exchange(chooser, tokens, grads, act_basis, grad_basis)
    return moment(grad_sq, act_sq, token_total)


def solution(mesh):
    placed = (
        P("dp", None),
        P(None, "dp", "owner"),
        P(None, "owner", "dp"),
        P(None, "dp", "owner"),
        P("dp", None),
    )
    return jax.shard_map(
        per_device, mesh=mesh, in_specs=placed, out_specs=P(None, "dp", "owner"), check_vma=False
    )
```
